32 devices in a mesh: rep: 4 (over z), member: 8 (over y, x, core).
Axes of the slice: x: 2, y: 2, z: 4, core: 2. Of those that a mesh axis runs over, the one named last changes fastest.
Arguments:
- acts: bfloat16 [512, 2, 100, 128], P(('rep', 'member')), may hold values from -6 to 6
- cotangent: bfloat16 [512, 2, 100, 128], P(('rep', 'member')), may hold values from -6 to 6
- routes: int32 [512, 2], P(('rep', 'member')), may hold values from 0 to 7, all different within a row; in each aligned block of 16 rows (0 to 15, 16 to 31, ...) at most 8 rows name the same one
- w_first: bfloat16 [8, 1152, 128], P('member'), may hold values from -0.1875 to 0.1875
- w_second: bfloat16 [8, 1152, 128], P('member'), may hold values from -0.1875 to 0.1875
- b_first: float32 [8, 128], P('member'), may hold values from -3 to 3
- b_second: float32 [8, 128], P('member'), may hold values from -3 to 3
Outputs:
- out_acts: bfloat16 [512, 2, 100, 128], P(('rep', 'member'))
- grad_acts: bfloat16 [512, 2, 100, 128], P(('rep', 'member'))
- grad_w_first: float32 [8, 1152, 128], P('member')
- grad_w_second: float32 [8, 1152, 128], P('member')
- grad_b_first: float32 [8, 128], P('member')
- grad_b_second: float32 [8, 128], P('member')
The draws below stay inside these ranges and needn't reach their ends.
Inputs may be any that keep to these rules, and one draw needn't show every extreme that they name: `routes`: the two members of a state differ. Among the 16 states of one device no member is named more than 8 times, and in some device one member is named exactly 8 times. Every member is named by some state.
All inputs are finite; a program needn't handle non-finite values.
Results may differ from the reference program's by a relative error of at most 0.007.
Values may be sent and summed in bfloat16 or wider, within the bound.
A program may use at most 64 MiB of HBM per device.

```python
import math
import jax
import jax.numpy as jnp
import numpy as np
from jax import lax

CH = 128
BOARD = 10
S_DEV = 16
CELLS = 100
MEMBERS = 8
CAP = 8
STATES = 512


def block_levels(stream_key, dims, pieces, least, high):
    def one(axis_at, shards_of):
        heights = jax.random.uniform(jax.random.fold_in(jax.random.fold_in(stream_key, 6), axis_at), (shards_of,), jnp.float32, least / len(pieces), high / len(pieces))
        return jnp.repeat(jnp.exp(heights), dims[axis_at] // shards_of).reshape((-1,) + (1,) * (len(dims) - axis_at - 1))

    level = one(*pieces[0])
    for cut in pieces[1:]:
        level = level * one(*cut)
    return level


def assign_block(stream_key, own, number, rows, amount, top, bound, skew):
    ranking = jax.random.permutation(stream_key, amount)
    crowded, usual = shares(amount, rows * top, bound, skew, True), shares(amount, rows * top, bound, skew, False)
    places = jnp.arange(amount)

    def named(tallies, rotation):
        used = int((tallies > 0).sum())
        fixed = max(1, used // 4)
        moved = fixed + (places - fixed + rotation * (used - fixed)) % max(1, amount - fixed)
        return jnp.zeros((amount,), jnp.int32).at[ranking[jnp.where(places < fixed, places, moved)]].set(jnp.asarray(tallies, jnp.int32))

    tallies = jnp.where(number % 4 == 0, named(crowded, number // 4), named(usual, number - number // 4 - 1))
    mixed = jax.random.permutation(jax.random.fold_in(own, 3), amount)
    giver, sink = mixed[0:amount // 2 * 2:2], mixed[1:amount // 2 * 2:2]
    margin = jnp.minimum(tallies[giver] - 1, bound - tallies[sink]) // 2
    margin = jnp.where((giver == ranking[0]) | (sink == ranking[0]) | (tallies[sink] == 0), 0, jnp.maximum(margin, 0))
    moved = jax.random.randint(jax.random.fold_in(own, 4), (amount // 2,), 0, 1 << 20) % (margin + 1)
    tallies = tallies.at[giver].add(-moved).at[sink].add(moved)
    members = jnp.searchsorted(jnp.cumsum(tallies), jnp.arange(rows * top), side="right").astype(jnp.int32)
    grid = members.reshape(top, rows).T
    grid = grid[jax.random.permutation(jax.random.fold_in(own, 1), rows)]
    rotation = jax.random.randint(jax.random.fold_in(own, 2), (rows, 1), 0, top)
    return jnp.take_along_axis(grid, (jnp.arange(top)[None, :] + rotation) % top, axis=1)


def shares(number_of, total, limit, lean, full):
    portions = [(1 << 20) // math.isqrt(rank ** lean) + 1 for rank in range(1, number_of + 1)]
    largest = limit if full else min(limit, max(-(-total // number_of), total * portions[0] // sum(portions)))
    least = 1 if total - largest >= number_of - 1 else 0
    counts, spare = [largest] + [least] * (number_of - 1), total - largest - least * (number_of - 1)
    while spare > 0:
        candidates = [i for i in range(1, number_of) if counts[i] < largest] or [i for i in range(1, number_of) if counts[i] < limit]
        whole, budget = sum([portions[i] for i in candidates]), spare
        for i in candidates:
            addition = min(limit - counts[i], max(1, budget * portions[i] // whole), spare)
            counts[i] = counts[i] + addition
            spare = spare - addition
    return np.array(counts)


def centred(rng, extent, spread, limit, cuts=(), kind=jnp.bfloat16):
    factor_of = block_levels(rng, extent, cuts, -0.22, 0.18) if cuts else 1.0
    values = jax.random.normal(rng, extent, jnp.float32) * spread * factor_of
    return jnp.minimum(jnp.maximum(values, -limit), limit).astype(kind)


def setup_inputs(seed: int = 0) -> dict:
    seeds = jax.random.split(jax.random.key(seed), 8)
    acts = centred(seeds[0], (STATES, 2, CELLS, CH), 1.0, 6.0, ((0, 32),))
    cotangent = centred(seeds[1], (STATES, 2, CELLS, CH), 1.0, 6.0, ((0, 32),))
    routes_keys = jax.random.split(jax.random.fold_in(seeds[2], 1), STATES // S_DEV)
    routes_turns = jax.random.permutation(jax.random.fold_in(seeds[2], 3), STATES // S_DEV)
    routes = jax.vmap(lambda own, number: assign_block(jax.random.fold_in(seeds[2], 2), own, number, S_DEV, MEMBERS, 2, CAP, 2))(routes_keys, routes_turns).reshape((STATES, 2))
    w_first = centred(seeds[3], (MEMBERS, 9 * CH, CH), (9 * CH) ** -0.5, 0.1875, ((0, 8),))
    w_second = centred(seeds[4], (MEMBERS, 9 * CH, CH), (9 * CH) ** -0.5, 0.1875, ((0, 8),))
    b_first = centred(seeds[5], (MEMBERS, CH), 0.5, 3.0, ((0, 8),), jnp.float32)
    b_second = centred(seeds[6], (MEMBERS, CH), 0.5, 3.0, ((0, 8),), jnp.float32)
    return dict(acts=acts, cotangent=cotangent, routes=routes, w_first=w_first, w_second=w_second, b_first=b_first, b_second=b_second)


def patches(values):
    leading = values.shape[:-2]
    channels = values.shape[-1]
    board_view = values.reshape(leading + (BOARD, BOARD, channels))
    padded = jnp.pad(board_view, [(0, 0)] * len(leading) + [(1, 1), (1, 1), (0, 0)])
    shifted = [padded[..., row_off:row_off + BOARD, col_off:col_off + BOARD, :] for row_off in range(3) for col_off in range(3)]
    return jnp.concatenate(shifted, axis=-1).reshape(leading + (BOARD * BOARD, 9 * channels))


def flipped(weight):
    channels = weight.shape[-1]
    stacked = weight.reshape(weight.shape[:-2] + (9, channels, channels))
    reversed_taps = jnp.flip(stacked, axis=-3)
    return jnp.swapaxes(reversed_taps, -1, -2).reshape(weight.shape)


def silu_slope(pre_act):
    sigmoid_vals = jax.nn.sigmoid(pre_act)
    return sigmoid_vals * (1.0 + pre_act * (1.0 - sigmoid_vals))


def reference(acts, cotangent, routes, w_first, w_second, b_first, b_second):
    inputs = acts.reshape(-1, CELLS, CH)
    upstream = cotangent.reshape(-1, CELLS, CH)
    member_ids = routes.reshape(-1).astype(jnp.int32)
    block_rows = 16
    num_blocks = inputs.shape[0] // block_rows
    highest = lax.Precision.HIGHEST

    def one_block(running, block_num):
        start = (block_num * block_rows).astype(jnp.int32)
        states_blk = lax.dynamic_slice_in_dim(inputs, start, block_rows, 0)
        upstream_blk = lax.dynamic_slice_in_dim(upstream, start, block_rows, 0)
        ids_blk = lax.dynamic_slice_in_dim(member_ids, start, block_rows, 0)
        weight_one = w_first[ids_blk].astype(jnp.float32)
        weight_two = w_second[ids_blk].astype(jnp.float32)
        in_patch = patches(states_blk).astype(jnp.float32)
        pre_act = jnp.einsum("rpk,rkc->rpc", in_patch, weight_one, precision=highest) + b_first[ids_blk][:, None, :]
        hidden = jax.nn.silu(pre_act).astype(jnp.bfloat16)
        hid_patch = patches(hidden).astype(jnp.float32)
        result = (states_blk.astype(jnp.float32) + jnp.einsum("rpk,rkc->rpc", hid_patch, weight_two, precision=highest) + b_second[ids_blk][:, None, :]).astype(jnp.bfloat16)
        grad_up = upstream_blk.astype(jnp.float32)
        grad_two = jnp.einsum("rpk,rpc->rkc", hid_patch, grad_up, precision=highest)
        bias_two = jnp.sum(grad_up, axis=1)
        up_patch = patches(upstream_blk).astype(jnp.float32)
        hidden_grad = jnp.einsum("rpk,rkc->rpc", up_patch, flipped(weight_two), precision=highest)
        pre_grad = (hidden_grad * silu_slope(pre_act)).astype(jnp.bfloat16)
        pre_grad_f = pre_grad.astype(jnp.float32)
        grad_one = jnp.einsum("rpk,rpc->rkc", in_patch, pre_grad_f, precision=highest)
        bias_one = jnp.sum(pre_grad_f, axis=1)
        delta_patch = patches(pre_grad).astype(jnp.float32)
        input_grad = (grad_up + jnp.einsum("rpk,rkc->rpc", delta_patch, flipped(weight_one), precision=highest)).astype(jnp.bfloat16)
        total_one, total_two, total_b_one, total_b_two = running
        running = (total_one.at[ids_blk].add(grad_one), total_two.at[ids_blk].add(grad_two),
                   total_b_one.at[ids_blk].add(bias_one), total_b_two.at[ids_blk].add(bias_two))
        return running, (result, input_grad)

    initial = (jnp.zeros((MEMBERS, 9 * CH, CH), jnp.float32), jnp.zeros((MEMBERS, 9 * CH, CH), jnp.float32),
               jnp.zeros((MEMBERS, CH), jnp.float32), jnp.zeros((MEMBERS, CH), jnp.float32))
    running, (results, input_grads) = lax.scan(one_block, initial, jnp.arange(num_blocks, dtype=jnp.int32))
    return (results.reshape(acts.shape), input_grads.reshape(acts.shape),
            running[0], running[1], running[2], running[3])
```

```python
import functools

import jax
import jax.numpy as jnp
from jax import lax
from jax.experimental import pallas as pl
from jax.experimental.pallas import tpu as pltpu
from jax.sharding import PartitionSpec as P

BOARD = 10


def flipped(weight):
    channels = weight.shape[-1]
    stacked = weight.reshape(weight.shape[:-2] + (9, channels, channels))
    reversed_taps = jnp.flip(stacked, axis=-3)
    return jnp.swapaxes(reversed_taps, -1, -2).reshape(weight.shape)


def silu_slope(pre_act):
    sigmoid_vals = jax.nn.sigmoid(pre_act)
    return sigmoid_vals * (1.0 + pre_act * (1.0 - sigmoid_vals))


def board_conv(values, weight):
    count = values.shape[0]
    channels = values.shape[-1]
    side = BOARD
    boards = values.reshape(count, side, side, channels)
    kernel = weight.reshape(3, 3, channels, channels)
    result = lax.conv_general_dilated(
        boards,
        kernel,
        (1, 1),
        ((1, 1), (1, 1)),
        dimension_numbers=("NHWC", "HWIO", "NHWC"),
        preferred_element_type=jnp.float32,
    )
    return result.reshape(count, side * side, channels)


def weight_conv(values, grads):
    count = values.shape[0]
    channels = values.shape[-1]
    side = BOARD
    boards = values.reshape(count, side, side, channels)
    grad_boards = grads.reshape(count, side, side, channels)
    result = lax.conv_general_dilated(
        boards,
        grad_boards,
        (1, 1),
        ((1, 1), (1, 1)),
        dimension_numbers=("CHWN", "IHWO", "NHWC"),
        preferred_element_type=jnp.float32,
    )
    return jnp.transpose(result, (1, 2, 0, 3)).reshape(9 * channels, channels)


def shards(acts, cotangent, routes, w_first, w_second, b_first, b_second):
    per_owner = w_first.shape[0]
    owners = lax.axis_size("member")
    members_all = owners * per_owner
    capacity = max(2, 4 * routes.shape[0] // members_all)
    channels = acts.shape[-1]
    cell_count = acts.shape[-2]
    member_ids = routes.reshape(-1)
    onehot = (member_ids[:, None] == jnp.arange(members_all, dtype=jnp.int32)[None, :]).astype(
        jnp.int32
    )
    order = jnp.arange(member_ids.shape[0], dtype=jnp.int32)
    earlier = jnp.sum((order[:, None] > order[None, :])[:, :, None] * onehot[None], axis=1)
    slot_index = jnp.sum(earlier * onehot, axis=1)
    target = member_ids * capacity + slot_index
    dispatch = (
        jnp.arange(members_all * capacity, dtype=jnp.int32)[:, None] == target[None, :]
    ).astype(jnp.bfloat16)

    def scatter_rows(values):
        flattened = values.reshape(-1, cell_count * channels)
        placed = jnp.dot(dispatch, flattened, preferred_element_type=jnp.float32).astype(
            jnp.bfloat16
        )
        return placed.reshape(members_all, capacity, cell_count, channels)

    def gather_rows(values):
        flattened = values.reshape(members_all * capacity, cell_count * channels)
        picked = jnp.dot(dispatch.T, flattened, preferred_element_type=jnp.float32).astype(
            jnp.bfloat16
        )
        return picked.reshape(acts.shape)

    def to_local(received):
        grouped = received.reshape(owners, per_owner, capacity, cell_count, channels)
        return jnp.swapaxes(grouped, 0, 1).reshape(
            per_owner, owners * capacity, cell_count, channels
        )

    def from_local(values):
        grouped = values.reshape(per_owner, owners, capacity, cell_count, channels)
        return jnp.swapaxes(grouped, 0, 1).reshape(members_all, capacity, cell_count, channels)

    send_acts = scatter_rows(acts)
    send_grads = scatter_rows(cotangent)
    recv_acts, recv_grads = (
        lax.all_to_all(send_acts, "member", split_axis=0, concat_axis=0, tiled=True),
        lax.all_to_all(send_grads, "member", split_axis=0, concat_axis=0, tiled=True),
    )
    inputs = to_local(recv_acts)
    upstream = to_local(recv_grads)
    owned = 0
    pre_one = board_conv(inputs[owned], w_first[owned]) + b_first[owned][None, None, :]
    hidden_one = jax.nn.silu(pre_one).astype(jnp.bfloat16)
    result_one = (
        inputs[owned].astype(jnp.float32)
        + board_conv(hidden_one, w_second[owned])
        + b_second[owned][None, None, :]
    ).astype(jnp.bfloat16)
    pre_list = [pre_one]
    hidden_list = [hidden_one]
    result_list = [result_one]
    result = jnp.stack(result_list)
    owned = 0
    upstream_one = upstream[owned]
    grad_two_list = [weight_conv(hidden_list[owned], upstream_one)]
    bias_two_list = [jnp.sum(upstream_one.astype(jnp.float32), axis=(0, 1))]
    hidden_grad = board_conv(upstream_one, flipped(w_second[owned]))
    pre_grad = (hidden_grad * silu_slope(pre_list[owned])).astype(jnp.bfloat16)
    grad_one_list = [weight_conv(inputs[owned], pre_grad)]
    bias_one_list = [jnp.sum(pre_grad.astype(jnp.float32), axis=(0, 1))]
    input_list = [
        (upstream_one.astype(jnp.float32) + board_conv(pre_grad, flipped(w_first[owned]))).astype(
            jnp.bfloat16
        )
    ]
    input_grad = jnp.stack(input_list)
    grad_one = jnp.stack(grad_one_list)
    grad_two = jnp.stack(grad_two_list)
    bias_one = jnp.stack(bias_one_list)
    bias_two = jnp.stack(bias_two_list)
    back_out, back_in = (
        lax.all_to_all(from_local(result), "member", split_axis=0, concat_axis=0, tiled=True),
        lax.all_to_all(from_local(input_grad), "member", split_axis=0, concat_axis=0, tiled=True),
    )
    totals = lax.psum((grad_one, grad_two, bias_one, bias_two), "rep")
    return (gather_rows(back_out), gather_rows(back_in), totals[0], totals[1], totals[2], totals[3])


SLOTS = 8
SIDE = BOARD + 2
CELLS = BOARD * BOARD
ROWS = CELLS * SLOTS
LINE = BOARD * SLOTS
TAIL = 64


def inner(line):
    return ((line + 1) * SIDE + 1) * SLOTS


def fill_patches(board_ref, patch_ref, channels):
    for tap in range(9):
        down, right = tap // 3, tap % 3
        for line in range(BOARD):
            start = ((line + down) * SIDE + right) * SLOTS
            patch_ref[line * LINE : (line + 1) * LINE, tap * channels : (tap + 1) * channels] = (
                board_ref[start : start + LINE, :].astype(jnp.bfloat16)
            )


def flipped_wide(weight_ref, base, channels):
    return jnp.concatenate(
        [
            weight_ref[base + (8 - tap) * channels : base + (9 - tap) * channels, :]
            for tap in range(9)
        ],
        axis=1,
    )


def tower_kernel(extra, slots_ref, acts_ref, cot_ref, weight_ref, *rest):
    rest = rest[extra:]
    (out_ref, back_ref, grads_ref, xs, gs, hs, ps, px, ph, pq, slope, flat_out, flat_back, stage, sems) = rest
    channels = weight_ref.shape[-1]
    taps = 9 * channels
    f32, bf16 = jnp.float32, jnp.bfloat16
    count = slots_ref[SLOTS]
    for ref in (xs, gs, hs, ps):
        ref[...] = jnp.zeros_like(ref)
    for slot in range(SLOTS):

        @pl.when(slot < count)
        def _():
            row = slots_ref[slot]
            for src, dst in ((acts_ref, xs), (cot_ref, gs)):
                board = src[row].astype(f32)
                for line in range(BOARD):
                    dst[pl.ds(inner(line) + slot, BOARD, stride=SLOTS), :] = board[
                        line * BOARD : (line + 1) * BOARD
                    ]

    def bias(at):
        return (
            weight_ref[2 * taps : 2 * taps + 16, :].astype(f32)[at : at + 3].sum(axis=0, keepdims=True)
        )

    def wide(lhs, rhs):
        return lax.dot_general(lhs, rhs, (((1,), (1,)), ((), ())), preferred_element_type=f32)

    def send_rows(which, flat, ref):
        for slot in range(SLOTS):

            @pl.when(slot < count)
            def _():
                stage[which * SLOTS + slot] = flat[pl.ds(slot, CELLS, stride=SLOTS), :].astype(bf16)
                pltpu.make_async_copy(
                    stage.at[which * SLOTS + slot],
                    ref.at[slots_ref[slot]],
                    sems.at[which * SLOTS + slot],
                ).start()

    fill_patches(xs, px, channels)
    pre = jnp.dot(px[...], weight_ref[:taps, :], preferred_element_type=f32) + bias(0)
    fill_patches(gs, pq, channels)
    hidden_grad = wide(pq[...], flipped_wide(weight_ref, taps, channels))
    gate = 0.5 * jnp.tanh(0.5 * pre) + 0.5
    slope[...] = hidden_grad * (gate * (1.0 + pre * (1.0 - gate)))
    hidden = (pre * gate).astype(bf16).astype(f32)
    for line in range(BOARD):
        hs[inner(line) : inner(line) + LINE, :] = hidden[line * LINE : (line + 1) * LINE]
    fill_patches(hs, ph, channels)

    flat_out[...] = jnp.dot(ph[...], weight_ref[taps : 2 * taps, :], preferred_element_type=f32) + bias(3)
    for line in range(BOARD):
        flat_out[line * LINE : (line + 1) * LINE, :] += xs[inner(line) : inner(line) + LINE, :]

    def weight_grad(grad, patch_ref, base):
        turned = wide_grad(grad, patch_ref)
        for tap in range(9):
            grads_ref[base + tap * channels : base + (tap + 1) * channels, :] = turned[
                :, tap * channels : (tap + 1) * channels
            ].astype(bf16)

    def wide_grad(grad, patch_ref):
        return jnp.dot(grad.T.astype(bf16), patch_ref[...], preferred_element_type=f32)

    upstream = jnp.concatenate(
        [gs[inner(line) : inner(line) + LINE, :] for line in range(BOARD)], axis=0
    )
    weight_grad(upstream, ph, taps)
    bias_two = jnp.sum(upstream, axis=0, keepdims=True)

    pre_grad = slope[...].astype(bf16).astype(f32)
    for line in range(BOARD):
        ps[inner(line) : inner(line) + LINE, :] = pre_grad[line * LINE : (line + 1) * LINE]
    fill_patches(ps, pq, channels)
    bias_one = jnp.sum(pre_grad, axis=0, keepdims=True)
    flat_back[...] = wide(pq[...], flipped_wide(weight_ref, 0, channels))
    for line in range(BOARD):
        flat_back[line * LINE : (line + 1) * LINE, :] += gs[inner(line) : inner(line) + LINE, :]
    weight_grad(pre_grad, px, 0)

    place = lax.broadcasted_iota(jnp.int32, (TAIL, channels), 0)
    tail = jnp.zeros((TAIL, channels), f32)
    for at, value in ((0, bias_one), (2, bias_two)):
        high = value.astype(bf16).astype(f32)
        tail = jnp.where(place == at, high, tail)
        tail = jnp.where(place == at + 1, value - high, tail)
    grads_ref[2 * taps :, :] = tail.astype(bf16)
    send_rows(0, flat_out, out_ref)
    send_rows(1, flat_back, back_ref)

    for which, ref in ((0, out_ref), (1, back_ref)):
        for slot in range(SLOTS):

            @pl.when(slot < count)
            def _():
                pltpu.make_async_copy(
                    stage.at[which * SLOTS + slot],
                    ref.at[slots_ref[slot]],
                    sems.at[which * SLOTS + slot],
                ).wait()


def tower(slots, acts, cotangent, weight, previous, after):
    channels = acts.shape[-1]
    taps = 9 * channels
    first = previous is None
    extra = (0 if first else 2) + len(after)
    vmem = pl.BlockSpec(memory_space=pltpu.VMEM)
    anywhere = pl.BlockSpec(memory_space=pl.ANY)
    rows_shape = jax.ShapeDtypeStruct(acts.shape, acts.dtype)
    board = pltpu.VMEM((SIDE * SIDE * SLOTS, channels), jnp.float32)
    patch = pltpu.VMEM((ROWS, taps), jnp.bfloat16)
    square = pltpu.VMEM((ROWS, channels), jnp.float32)
    flops = 12 * ROWS * taps * channels
    return pl.pallas_call(
        functools.partial(tower_kernel, extra),
        out_shape=(
            rows_shape,
            rows_shape,
            jax.ShapeDtypeStruct((2 * taps + TAIL, channels), jnp.bfloat16),
        ),
        in_specs=[pl.BlockSpec(memory_space=pltpu.SMEM), vmem, vmem, vmem]
        + [anywhere] * extra,
        out_specs=(anywhere, anywhere, vmem),
        scratch_shapes=[board] * 4
        + [patch] * 3
        + [square] * 3
        + [
            pltpu.VMEM((2 * SLOTS, CELLS, channels), jnp.bfloat16),
            pltpu.SemaphoreType.DMA((2 * SLOTS,)),
        ],
        input_output_aliases={} if first else {4: 0, 5: 1},
        compiler_params=pltpu.CompilerParams(vmem_limit_bytes=40 * 1024 * 1024),
        cost_estimate=pl.CostEstimate(flops=6 * flops, bytes_accessed=4000000, transcendentals=ROWS * channels),
        name="tower",
    )(slots, acts, cotangent, weight, *(() if first else previous), *after)


def parts_of(value):
    high = lax.reduce_precision(value, 8, 7)
    middle = lax.reduce_precision(value - high, 8, 7)
    return [high, middle, value - high - middle]


def at_home(acts, cotangent, routes, w_first, w_second, b_first, b_second):
    owners = lax.axis_size("member")
    copies = lax.axis_size("rep")
    channels = acts.shape[-1]
    taps = 9 * channels
    me = lax.axis_index("member")
    member_ids = routes.reshape(-1)
    total = member_ids.shape[0]
    named = member_ids[None, :] == jnp.arange(owners, dtype=jnp.int32)[:, None]
    counts = jnp.sum(named.astype(jnp.int32), axis=1)
    order = jnp.arange(total, dtype=jnp.int32)
    before = (order[:, None] > order[None, :]) & named[:, None, :]
    place = jnp.sum(before.astype(jnp.int32), axis=2)
    hit = named[:, None, :] & (
        place[:, None, :] == jnp.arange(SLOTS, dtype=jnp.int32)[None, :, None]
    )
    rows = jnp.sum(jnp.where(hit, jnp.arange(total, dtype=jnp.int32)[None, None, :], 0), axis=2)
    table = jnp.concatenate([rows, counts[:, None]], axis=1)

    x = acts.reshape((total,) + acts.shape[2:])
    g = cotangent.reshape((total,) + acts.shape[2:])
    pieces = parts_of(b_first) + parts_of(b_second)
    bias_tile = jnp.concatenate(
        [piece.astype(jnp.bfloat16) for piece in pieces]
        + [jnp.zeros((10, channels), jnp.bfloat16)],
        axis=0,
    )
    own = jnp.concatenate([w_first[0], w_second[0], lax.optimization_barrier(bias_tile)], axis=0)

    def swap(value, offset, axis="member"):
        size = lax.axis_size(axis)
        return lax.ppermute(value, axis, [(i, i ^ offset) for i in range(size)])

    chips = owners // 2
    same = [own] + [swap(own, 2 * step) for step in range(1, chips)]
    other = [swap(value, 1) for value in same]
    previous = None
    summed = None
    after = ()
    totals = []
    held = []
    for step in range(chips):
        made = {}
        order = (0, 1) if step == 0 else (1, 0)
        for side in order:
            weight = (same, other)[side][step]
            member = me ^ (2 * step + side)
            slots = lax.dynamic_index_in_dim(table, member, 0, keepdims=False)
            out, back, grads = tower(slots, x, g, weight, previous, after)
            after = ()
            previous = (out, back)
            made[side] = grads
        pair = made[0].astype(jnp.float32) + swap(made[1], 1).astype(jnp.float32)
        if step == 0:
            totals.append(pair)
        else:
            narrow = pair.astype(jnp.bfloat16)
            totals.append(swap(narrow, 2 * step).astype(jnp.float32))
            held.append(narrow)
        if held:
            after = (held.pop(),)
    summed = sum(totals[1:], totals[0])

    rep = lax.axis_index("rep")
    chunks = summed.reshape(copies, summed.shape[0] // copies, channels)
    sends = chunks.astype(jnp.bfloat16)
    mine = lax.dynamic_index_in_dim(chunks, rep, 0, keepdims=False)
    for far in range(1, copies):
        sent = lax.dynamic_index_in_dim(sends, rep ^ far, 0, keepdims=False)
        mine = mine + swap(sent, far, "rep").astype(jnp.float32)
    mine = mine.astype(jnp.bfloat16)
    gathered = [mine] + [swap(mine, far, "rep") for far in range(1, copies)]
    offset = 1
    while offset < copies:
        odd = (rep & offset) != 0
        gathered = [
            jnp.where(odd, gathered[at ^ offset], gathered[at]) for at in range(copies)
        ]
        offset *= 2
    summed = jnp.concatenate(gathered, axis=0).astype(jnp.float32)

    def turned(part):
        return jnp.swapaxes(part.reshape(9, channels, channels), 1, 2).reshape(1, taps, channels)

    tail = summed[2 * taps :]
    return (
        previous[0].reshape(acts.shape),
        previous[1].reshape(acts.shape),
        turned(summed[:taps]),
        turned(summed[taps : 2 * taps]),
        (tail[0] + tail[1])[None],
        (tail[2] + tail[3])[None],
    )


def solution(mesh):
    placed = (
        P(("rep", "member"), None, None, None),
        P(("rep", "member"), None, None, None),
        P(("rep", "member"), None),
        P("member", None, None),
        P("member", None, None),
        P("member", None),
        P("member", None),
    )
    return jax.shard_map(
        at_home if mesh.shape["member"] <= 8 else shards,
        mesh=mesh,
        in_specs=placed,
        out_specs=(
            P(("rep", "member"), None, None, None),
            P(("rep", "member"), None, None, None),
            P("member", None, None),
            P("member", None, None),
            P("member", None),
            P("member", None),
        ),
        check_vma=False,
    )
```

```python
import functools

import jax
import jax.numpy as jnp
from jax import lax
from jax.experimental import pallas as pl
from jax.experimental.pallas import tpu as pltpu
from jax.sharding import PartitionSpec as P

BOARD = 10


def flipped(weight):
    channels = weight.shape[-1]
    stacked = weight.reshape(weight.shape[:-2] + (9, channels, channels))
    reversed_taps = jnp.flip(stacked, axis=-3)
    return jnp.swapaxes(reversed_taps, -1, -2).reshape(weight.shape)


def silu_slope(pre_act):
    sigmoid_vals = jax.nn.sigmoid(pre_act)
    return sigmoid_vals * (1.0 + pre_act * (1.0 - sigmoid_vals))


def board_conv(values, weight):
    count = values.shape[0]
    channels = values.shape[-1]
    side = BOARD
    boards = values.reshape(count, side, side, channels)
    kernel = weight.reshape(3, 3, channels, channels)
    result = lax.conv_general_dilated(
        boards,
        kernel,
        (1, 1),
        ((1, 1), (1, 1)),
        dimension_numbers=("NHWC", "HWIO", "NHWC"),
        preferred_element_type=jnp.float32,
    )
    return result.reshape(count, side * side, channels)


def weight_conv(values, grads):
    count = values.shape[0]
    channels = values.shape[-1]
    side = BOARD
    boards = values.reshape(count, side, side, channels)
    grad_boards = grads.reshape(count, side, side, channels)
    result = lax.conv_general_dilated(
        boards,
        grad_boards,
        (1, 1),
        ((1, 1), (1, 1)),
        dimension_numbers=("CHWN", "IHWO", "NHWC"),
        preferred_element_type=jnp.float32,
    )
    return jnp.transpose(result, (1, 2, 0, 3)).reshape(9 * channels, channels)


def shards(acts, cotangent, routes, w_first, w_second, b_first, b_second):
    per_owner = w_first.shape[0]
    owners = lax.axis_size("member")
    members_all = owners * per_owner
    capacity = max(2, 4 * routes.shape[0] // members_all)
    channels = acts.shape[-1]
    cell_count = acts.shape[-2]
    member_ids = routes.reshape(-1)
    onehot = (member_ids[:, None] == jnp.arange(members_all, dtype=jnp.int32)[None, :]).astype(
        jnp.int32
    )
    order = jnp.arange(member_ids.shape[0], dtype=jnp.int32)
    earlier = jnp.sum((order[:, None] > order[None, :])[:, :, None] * onehot[None], axis=1)
    slot_index = jnp.sum(earlier * onehot, axis=1)
    target = member_ids * capacity + slot_index
    dispatch = (
        jnp.arange(members_all * capacity, dtype=jnp.int32)[:, None] == target[None, :]
    ).astype(jnp.bfloat16)

    def scatter_rows(values):
        flattened = values.reshape(-1, cell_count * channels)
        placed = jnp.dot(dispatch, flattened, preferred_element_type=jnp.float32).astype(
            jnp.bfloat16
        )
        return placed.reshape(members_all, capacity, cell_count, channels)

    def gather_rows(values):
        flattened = values.reshape(members_all * capacity, cell_count * channels)
        picked = jnp.dot(dispatch.T, flattened, preferred_element_type=jnp.float32).astype(
            jnp.bfloat16
        )
        return picked.reshape(acts.shape)

    def to_local(received):
        grouped = received.reshape(owners, per_owner, capacity, cell_count, channels)
        return jnp.swapaxes(grouped, 0, 1).reshape(
            per_owner, owners * capacity, cell_count, channels
        )

    def from_local(values):
        grouped = values.reshape(per_owner, owners, capacity, cell_count, channels)
        return jnp.swapaxes(grouped, 0, 1).reshape(members_all, capacity, cell_count, channels)

    send_acts = scatter_rows(acts)
    send_grads = scatter_rows(cotangent)
    recv_acts, recv_grads = (
        lax.all_to_all(send_acts, "member", split_axis=0, concat_axis=0, tiled=True),
        lax.all_to_all(send_grads, "member", split_axis=0, concat_axis=0, tiled=True),
    )
    inputs = to_local(recv_acts)
    upstream = to_local(recv_grads)
    owned = 0
    pre_one = board_conv(inputs[owned], w_first[owned]) + b_first[owned][None, None, :]
    hidden_one = jax.nn.silu(pre_one).astype(jnp.bfloat16)
    result_one = (
        inputs[owned].astype(jnp.float32)
        + board_conv(hidden_one, w_second[owned])
        + b_second[owned][None, None, :]
    ).astype(jnp.bfloat16)
    pre_list = [pre_one]
    hidden_list = [hidden_one]
    result_list = [result_one]
    result = jnp.stack(result_list)
    owned = 0
    upstream_one = upstream[owned]
    grad_two_list = [weight_conv(hidden_list[owned], upstream_one)]
    bias_two_list = [jnp.sum(upstream_one.astype(jnp.float32), axis=(0, 1))]
    hidden_grad = board_conv(upstream_one, flipped(w_second[owned]))
    pre_grad = (hidden_grad * silu_slope(pre_list[owned])).astype(jnp.bfloat16)
    grad_one_list = [weight_conv(inputs[owned], pre_grad)]
    bias_one_list = [jnp.sum(pre_grad.astype(jnp.float32), axis=(0, 1))]
    input_list = [
        (upstream_one.astype(jnp.float32) + board_conv(pre_grad, flipped(w_first[owned]))).astype(
            jnp.bfloat16
        )
    ]
    input_grad = jnp.stack(input_list)
    grad_one = jnp.stack(grad_one_list)
    grad_two = jnp.stack(grad_two_list)
    bias_one = jnp.stack(bias_one_list)
    bias_two = jnp.stack(bias_two_list)
    back_out, back_in = (
        lax.all_to_all(from_local(result), "member", split_axis=0, concat_axis=0, tiled=True),
        lax.all_to_all(from_local(input_grad), "member", split_axis=0, concat_axis=0, tiled=True),
    )
    totals = lax.psum((grad_one, grad_two, bias_one, bias_two), "rep")
    return (gather_rows(back_out), gather_rows(back_in), totals[0], totals[1], totals[2], totals[3])


SLOTS = 8
SIDE = BOARD + 2
CELLS = BOARD * BOARD
ROWS = CELLS * SLOTS
LINE = BOARD * SLOTS
TAIL = 64


def inner(line):
    return ((line + 1) * SIDE + 1) * SLOTS


def fill_patches(board_ref, patch_ref, channels):
    for tap in range(9):
        down, right = tap // 3, tap % 3
        for line in range(BOARD):
            start = ((line + down) * SIDE + right) * SLOTS
            patch_ref[line * LINE : (line + 1) * LINE, tap * channels : (tap + 1) * channels] = (
                board_ref[start : start + LINE, :].astype(jnp.bfloat16)
            )


def flipped_wide(weight_ref, base, channels):
    return jnp.concatenate(
        [
            weight_ref[base + (8 - tap) * channels : base + (9 - tap) * channels, :]
            for tap in range(9)
        ],
        axis=1,
    )


def tower_kernel(extra, slots_ref, acts_ref, cot_ref, weight_ref, *rest):
    rest = rest[extra:]
    (out_ref, back_ref, grads_ref, xs, gs, hs, ps, px, ph, pq, slope, flat_out, flat_back, stage, sems) = rest
    channels = weight_ref.shape[-1]
    taps = 9 * channels
    f32, bf16 = jnp.float32, jnp.bfloat16
    count = slots_ref[SLOTS]
    for ref in (xs, gs, hs, ps):
        ref[...] = jnp.zeros_like(ref)
    for slot in range(SLOTS):

        @pl.when(slot < count)
        def _():
            row = slots_ref[slot]
            for src, dst in ((acts_ref, xs), (cot_ref, gs)):
                board = src[row].astype(f32)
                for line in range(BOARD):
                    dst[pl.ds(inner(line) + slot, BOARD, stride=SLOTS), :] = board[
                        line * BOARD : (line + 1) * BOARD
                    ]

    def bias(at):
        return (
            weight_ref[2 * taps : 2 * taps + 16, :].astype(f32)[at : at + 3].sum(axis=0, keepdims=True)
        )

    def wide(lhs, rhs):
        return lax.dot_general(lhs, rhs, (((1,), (1,)), ((), ())), preferred_element_type=f32)

    def send_rows(which, flat, ref):
        for slot in range(SLOTS):

            @pl.when(slot < count)
            def _():
                stage[which * SLOTS + slot] = flat[pl.ds(slot, CELLS, stride=SLOTS), :].astype(bf16)
                pltpu.make_async_copy(
                    stage.at[which * SLOTS + slot],
                    ref.at[slots_ref[slot]],
                    sems.at[which * SLOTS + slot],
                ).start()

    fill_patches(xs, px, channels)
    pre = jnp.dot(px[...], weight_ref[:taps, :], preferred_element_type=f32) + bias(0)
    fill_patches(gs, pq, channels)
    hidden_grad = wide(pq[...], flipped_wide(weight_ref, taps, channels))
    gate = 0.5 * jnp.tanh(0.5 * pre) + 0.5
    slope[...] = hidden_grad * (gate * (1.0 + pre * (1.0 - gate)))
    hidden = (pre * gate).astype(bf16).astype(f32)
    for line in range(BOARD):
        hs[inner(line) : inner(line) + LINE, :] = hidden[line * LINE : (line + 1) * LINE]
    fill_patches(hs, ph, channels)

    flat_out[...] = jnp.dot(ph[...], weight_ref[taps : 2 * taps, :], preferred_element_type=f32) + bias(3)
    for line in range(BOARD):
        flat_out[line * LINE : (line + 1) * LINE, :] += xs[inner(line) : inner(line) + LINE, :]

    def weight_grad(grad, patch_ref, base):
        turned = wide_grad(grad, patch_ref)
        for tap in range(9):
            grads_ref[base + tap * channels : base + (tap + 1) * channels, :] = turned[
                :, tap * channels : (tap + 1) * channels
            ].astype(bf16)

    def wide_grad(grad, patch_ref):
        return jnp.dot(grad.T.astype(bf16), patch_ref[...], preferred_element_type=f32)

    upstream = jnp.concatenate(
        [gs[inner(line) : inner(line) + LINE, :] for line in range(BOARD)], axis=0
    )
    weight_grad(upstream, ph, taps)
    bias_two = jnp.sum(upstream, axis=0, keepdims=True)

    pre_grad = slope[...].astype(bf16).astype(f32)
    for line in range(BOARD):
        ps[inner(line) : inner(line) + LINE, :] = pre_grad[line * LINE : (line + 1) * LINE]
    fill_patches(ps, pq, channels)
    bias_one = jnp.sum(pre_grad, axis=0, keepdims=True)
    flat_back[...] = wide(pq[...], flipped_wide(weight_ref, 0, channels))
    for line in range(BOARD):
        flat_back[line * LINE : (line + 1) * LINE, :] += gs[inner(line) : inner(line) + LINE, :]
    weight_grad(pre_grad, px, 0)

    place = lax.broadcasted_iota(jnp.int32, (TAIL, channels), 0)
    tail = jnp.zeros((TAIL, channels), f32)
    for at, value in ((0, bias_one), (2, bias_two)):
        high = value.astype(bf16).astype(f32)
        tail = jnp.where(place == at, high, tail)
        tail = jnp.where(place == at + 1, value - high, tail)
    grads_ref[2 * taps :, :] = tail.astype(bf16)
    send_rows(0, flat_out, out_ref)
    send_rows(1, flat_back, back_ref)

    for which, ref in ((0, out_ref), (1, back_ref)):
        for slot in range(SLOTS):

            @pl.when(slot < count)
            def _():
                pltpu.make_async_copy(
                    stage.at[which * SLOTS + slot],
                    ref.at[slots_ref[slot]],
                    sems.at[which * SLOTS + slot],
                ).wait()


def tower(slots, acts, cotangent, weight, previous, after):
    channels = acts.shape[-1]
    taps = 9 * channels
    first = previous is None
    extra = (0 if first else 2) + len(after)
    vmem = pl.BlockSpec(memory_space=pltpu.VMEM)
    anywhere = pl.BlockSpec(memory_space=pl.ANY)
    rows_shape = jax.ShapeDtypeStruct(acts.shape, acts.dtype)
    board = pltpu.VMEM((SIDE * SIDE * SLOTS, channels), jnp.float32)
    patch = pltpu.VMEM((ROWS, taps), jnp.bfloat16)
    square = pltpu.VMEM((ROWS, channels), jnp.float32)
    flops = 12 * ROWS * taps * channels
    return pl.pallas_call(
        functools.partial(tower_kernel, extra),
        out_shape=(
            rows_shape,
            rows_shape,
            jax.ShapeDtypeStruct((2 * taps + TAIL, channels), jnp.bfloat16),
        ),
        in_specs=[pl.BlockSpec(memory_space=pltpu.SMEM), vmem, vmem, vmem]
        + [anywhere] * extra,
        out_specs=(anywhere, anywhere, vmem),
        scratch_shapes=[board] * 4
        + [patch] * 3
        + [square] * 3
        + [
            pltpu.VMEM((2 * SLOTS, CELLS, channels), jnp.bfloat16),
            pltpu.SemaphoreType.DMA((2 * SLOTS,)),
        ],
        input_output_aliases={} if first else {4: 0, 5: 1},
        compiler_params=pltpu.CompilerParams(vmem_limit_bytes=40 * 1024 * 1024),
        cost_estimate=pl.CostEstimate(flops=6 * flops, bytes_accessed=4000000, transcendentals=ROWS * channels),
        name="tower",
    )(slots, acts, cotangent, weight, *(() if first else previous), *after)


def parts_of(value):
    high = lax.reduce_precision(value, 8, 7)
    middle = lax.reduce_precision(value - high, 8, 7)
    return [high, middle, value - high - middle]


def at_home(acts, cotangent, routes, w_first, w_second, b_first, b_second):
    owners = lax.axis_size("member")
    copies = lax.axis_size("rep")
    channels = acts.shape[-1]
    taps = 9 * channels
    me = lax.axis_index("member")
    member_ids = routes.reshape(-1)
    total = member_ids.shape[0]
    named = member_ids[None, :] == jnp.arange(owners, dtype=jnp.int32)[:, None]
    counts = jnp.sum(named.astype(jnp.int32), axis=1)
    order = jnp.arange(total, dtype=jnp.int32)
    before = (order[:, None] > order[None, :]) & named[:, None, :]
    place = jnp.sum(before.astype(jnp.int32), axis=2)
    hit = named[:, None, :] & (
        place[:, None, :] == jnp.arange(SLOTS, dtype=jnp.int32)[None, :, None]
    )
    rows = jnp.sum(jnp.where(hit, jnp.arange(total, dtype=jnp.int32)[None, None, :], 0), axis=2)
    table = jnp.concatenate([rows, counts[:, None]], axis=1)

    x = acts.reshape((total,) + acts.shape[2:])
    g = cotangent.reshape((total,) + acts.shape[2:])
    pieces = parts_of(b_first) + parts_of(b_second)
    bias_tile = jnp.concatenate(
        [piece.astype(jnp.bfloat16) for piece in pieces]
        + [jnp.zeros((10, channels), jnp.bfloat16)],
        axis=0,
    )
    own = jnp.concatenate([w_first[0], w_second[0], lax.optimization_barrier(bias_tile)], axis=0)

    def swap(value, offset, axis="member"):
        size = lax.axis_size(axis)
        return lax.ppermute(value, axis, [(i, i ^ offset) for i in range(size)])

    chips = owners // 2
    same = [own] + [swap(own, 2 * step) for step in range(1, chips)]
    other = [swap(value, 1) for value in same]
    previous = None
    summed = None
    after = ()
    totals = []
    held = []
    last = None
    for step in range(chips):
        made = {}
        order = (0, 1) if step == 0 else (1, 0)
        for side in order:
            weight = (same, other)[side][step]
            member = me ^ (2 * step + side)
            slots = lax.dynamic_index_in_dim(table, member, 0, keepdims=False)
            out, back, grads = tower(slots, x, g, weight, previous, after)
            after = ()
            previous = (out, back)
            made[side] = grads
        pair = made[0].astype(jnp.float32) + swap(made[1], 1).astype(jnp.float32)
        if step == 0:
            totals.append(pair)
        elif step == chips - 1:
            last = pair
        else:
            narrow = pair.astype(jnp.bfloat16)
            totals.append(swap(narrow, 2 * step).astype(jnp.float32))
            held.append(narrow)
        if held:
            after = (held.pop(),)

    rep = lax.axis_index("rep")

    def scattered(value):
        chunks = value.reshape(copies, value.shape[0] // copies, channels)
        sends = chunks.astype(jnp.bfloat16)
        mine = lax.dynamic_index_in_dim(chunks, rep, 0, keepdims=False)
        for far in range(1, copies):
            sent = lax.dynamic_index_in_dim(sends, rep ^ far, 0, keepdims=False)
            mine = mine + swap(sent, far, "rep").astype(jnp.float32)
        return mine

    mine = 0.0
    if last is not None:
        mine = swap(scattered(last).astype(jnp.bfloat16), 2 * (chips - 1)).astype(jnp.float32)
    mine = mine + scattered(sum(totals[1:], totals[0]))
    mine = mine.astype(jnp.bfloat16)
    gathered = [mine] + [swap(mine, far, "rep") for far in range(1, copies)]
    offset = 1
    while offset < copies:
        odd = (rep & offset) != 0
        gathered = [
            jnp.where(odd, gathered[at ^ offset], gathered[at]) for at in range(copies)
        ]
        offset *= 2
    summed = jnp.concatenate(gathered, axis=0).astype(jnp.float32)

    def turned(part):
        return jnp.swapaxes(part.reshape(9, channels, channels), 1, 2).reshape(1, taps, channels)

    tail = summed[2 * taps :]
    return (
        previous[0].reshape(acts.shape),
        previous[1].reshape(acts.shape),
        turned(summed[:taps]),
        turned(summed[taps : 2 * taps]),
        (tail[0] + tail[1])[None],
        (tail[2] + tail[3])[None],
    )


def solution(mesh):
    placed = (
        P(("rep", "member"), None, None, None),
        P(("rep", "member"), None, None, None),
        P(("rep", "member"), None),
        P("member", None, None),
        P("member", None, None),
        P("member", None),
        P("member", None),
    )
    return jax.shard_map(
        at_home if mesh.shape["member"] <= 8 else shards,
        mesh=mesh,
        in_specs=placed,
        out_specs=(
            P(("rep", "member"), None, None, None),
            P(("rep", "member"), None, None, None),
            P("member", None, None),
            P("member", None, None),
            P("member", None),
            P("member", None),
        ),
        check_vma=False,
    )
```
